128 devices in a mesh: ctx: 32 (over z, x, core), rep: 4 (over y).
Axes of the slice: x: 4, y: 4, z: 4, core: 2. Of those that a mesh axis runs over, the one named last changes fastest.
Arguments:
- query: bfloat16 [49152, 4096], P(('rep', 'ctx')), parts along dimension 0, may hold values from -6 to 6
- key: bfloat16 [49152, 4096], P(('rep', 'ctx')), parts along dimension 0, may hold values from -6 to 6
- value: bfloat16 [49152, 4096], P(('rep', 'ctx')), parts along dimension 0, may hold values from -6 to 6
- output: bfloat16 [49152, 4096], P(('rep', 'ctx')), parts along dimension 0, may hold values from -6 to 6
- grad_out: bfloat16 [49152, 4096], P(('rep', 'ctx')), parts along dimension 0, may hold values from -96 to 96
- lse: float32 [32, 49152], P(None, ('rep', 'ctx')), parts along dimension 1, may hold values from 6.5 to 8.5
Outputs:
- grad_query: bfloat16 [49152, 4096], P(('rep', 'ctx')), parts along dimension 0
- grad_key: bfloat16 [49152, 4096], P(('rep', 'ctx')), parts along dimension 0
- grad_value: bfloat16 [49152, 4096], P(('rep', 'ctx')), parts along dimension 0
The draws below stay inside these ranges and needn't reach their ends.
There are 4 independent parts, one for each index of `rep`. The reference program is written for one: setup_inputs(seed, part) draws one part's arguments, and reference() takes and returns one part's arrays. A program takes and returns all parts, laid end to end along the dimension named above; each array names one. Nothing has to cross between parts.
All inputs are finite; a program needn't handle non-finite values.
Results may differ from the reference program's by a relative error of at most 0.005.
Values may be sent and summed in bfloat16 or wider, within the bound.
No kernel may reach another device: no remote copies, remote signals or barrier semaphores. Data moves between devices by JAX's collectives and lax.ppermute only.
A program may use at most 256 MiB of HBM per device.

```python
import math
import jax
import jax.numpy as jnp
from jax import lax

HEADS = 32
HDIM = 128
WIDTH = 4096
TOK_DEV = 384
SEQ = 12288
NEAR = 8
FAR = 24
N_CTX = 32


def levels(rng, shape, cuts, low, largest):
    def one(dim, blocks):
        steps = jax.random.uniform(jax.random.fold_in(jax.random.fold_in(rng, 6), dim), (blocks,), jnp.float32, low / len(cuts), largest / len(cuts))
        return jnp.repeat(jnp.exp(steps), shape[dim] // blocks).reshape((-1,) + (1,) * (len(shape) - dim - 1))

    gain = one(*cuts[0])
    for cut in cuts[1:]:
        gain = gain * one(*cut)
    return gain


def bell_draw(key, dims, scale, bound, cuts=(), kind=jnp.bfloat16):
    result = scale * jax.random.normal(key, dims, jnp.float32)
    if cuts:
        result = result * levels(key, dims, cuts, -0.22, 0.18)
    return jnp.clip(result, -bound, bound).astype(kind)


def setup_inputs(seed: int = 0, part: int = 0) -> dict:
    seeds = jax.random.split(jax.random.key(seed), 7)
    part_splits = jax.random.split(jax.random.fold_in(seeds[6], part), 7)
    return {
        "query": bell_draw(part_splits[0], (SEQ, WIDTH), 1.0, 6.0, ((0, 32),)),
        "key": bell_draw(part_splits[1], (SEQ, WIDTH), 1.0, 6.0, ((0, 32),)),
        "value": bell_draw(part_splits[2], (SEQ, WIDTH), 1.0, 6.0, ((0, 32),)),
        "output": bell_draw(part_splits[3], (SEQ, WIDTH), 1.0, 6.0, ((0, 32),)),
        "grad_out": bell_draw(part_splits[4], (SEQ, WIDTH), 16.0, 96.0, ((0, 32),)),
        "lse": jnp.clip(6.5 + 2.0 * jax.random.uniform(part_splits[5], (HEADS, SEQ), jnp.float32) ** levels(part_splits[5], (HEADS, SEQ), ((1, 32),), -0.2, 0.2), 6.5, 8.5),
    }


def block_pair(q_block, dout_block, lse_block, delta_block, k_block, v_block, weight, causal):
    scale = 1.0 / math.sqrt(HDIM)
    q_full = q_block.astype(jnp.float32).reshape(TOK_DEV, HEADS, HDIM)
    d_full = dout_block.astype(jnp.float32).reshape(TOK_DEV, HEADS, HDIM)
    k_full = k_block.astype(jnp.float32).reshape(TOK_DEV, HEADS, HDIM)
    v_full = v_block.astype(jnp.float32).reshape(TOK_DEV, HEADS, HDIM)
    scores = jnp.einsum('thd,shd->hts', q_full, k_full) * scale
    prob = jnp.exp(scores - lse_block[:, :, None]) * weight
    if causal:
        lower = jnp.arange(TOK_DEV)[:, None] >= jnp.arange(TOK_DEV)[None, :]
        prob = jnp.where(lower[None, :, :], prob, jnp.zeros_like(prob))
    prob_half = lax.optimization_barrier(prob.astype(jnp.bfloat16))
    dprob = jnp.einsum('thd,shd->hts', d_full, v_full)
    dscore = lax.optimization_barrier((scale * prob * (dprob - delta_block[:, :, None])).astype(jnp.bfloat16))
    dscore_f = dscore.astype(jnp.float32)
    grad_q = jnp.einsum('hts,shd->thd', dscore_f, k_full).reshape(TOK_DEV, WIDTH)
    grad_k = jnp.einsum('hts,thd->shd', dscore_f, q_full).reshape(TOK_DEV, WIDTH)
    grad_v = jnp.einsum('hts,thd->shd', prob_half.astype(jnp.float32), d_full).reshape(TOK_DEV, WIDTH)
    return (grad_q, grad_k, grad_v)

def reference(query, key, value, output, grad_out, lse):
    delta = lax.optimization_barrier(jnp.sum((grad_out.astype(jnp.float32) * output.astype(jnp.float32)).reshape(SEQ, HEADS, HDIM), axis=2)).T
    q_blocks = query.reshape(N_CTX, TOK_DEV, WIDTH)
    d_blocks = grad_out.reshape(N_CTX, TOK_DEV, WIDTH)
    k_blocks = key.reshape(N_CTX, TOK_DEV, WIDTH)
    v_blocks = value.reshape(N_CTX, TOK_DEV, WIDTH)
    l_blocks = lse.reshape(HEADS, N_CTX, TOK_DEV).transpose(1, 0, 2)
    e_blocks = delta.reshape(HEADS, N_CTX, TOK_DEV).transpose(1, 0, 2)
    total_q = jnp.zeros((N_CTX, TOK_DEV, WIDTH), jnp.float32)
    total_k = jnp.zeros((N_CTX, TOK_DEV, WIDTH), jnp.float32)
    total_v = jnp.zeros((N_CTX, TOK_DEV, WIDTH), jnp.float32)
    for distance, causal in ((0, True), (NEAR, False), (FAR, False)):
        padding = jnp.zeros((distance, TOK_DEV, WIDTH), key.dtype)
        k_moved = jnp.concatenate([padding, k_blocks[:N_CTX - distance]], axis=0)
        v_moved = jnp.concatenate([padding, v_blocks[:N_CTX - distance]], axis=0)
        weight = (jnp.arange(N_CTX) >= distance).astype(jnp.float32)

        def one_block(items, causal=causal):
            return block_pair(*items, causal)
        grad_q, grad_k, grad_v = lax.map(one_block, (q_blocks, d_blocks, l_blocks, e_blocks, k_moved, v_moved, weight))
        empty = jnp.zeros((distance, TOK_DEV, WIDTH), jnp.float32)
        total_q = total_q + grad_q
        total_k = total_k + jnp.concatenate([grad_k[distance:], empty], axis=0)
        total_v = total_v + jnp.concatenate([grad_v[distance:], empty], axis=0)
    return (total_q.reshape(SEQ, WIDTH).astype(jnp.bfloat16), total_k.reshape(SEQ, WIDTH).astype(jnp.bfloat16), total_v.reshape(SEQ, WIDTH).astype(jnp.bfloat16))
```

```python
import math

import jax
import jax.numpy as jnp
from jax import lax
from jax.experimental import pallas as pl
from jax.experimental.pallas import tpu as pltpu
from jax.sharding import PartitionSpec as P

F32 = jnp.float32
BF16 = jnp.bfloat16
VMEM_BYTES = 56 * 1024 * 1024
CHUNKS = (4, 4, 8, 8, 4, 2, 2)
COST = 100
LOG2E = math.log2(math.e)
KEPT = pl.BlockSpec(memory_space=pl.ANY)
PARAMS = pltpu.CompilerParams(vmem_limit_bytes=VMEM_BYTES)


def dot_nt(a, b):
    return lax.dot_general(a, b, (((1,), (1,)), ((), ())), preferred_element_type=F32)


def dot_nn(a, b):
    return lax.dot_general(a, b, (((1,), (0,)), ((), ())), preferred_element_type=F32)


def dot_tn(a, b):
    return lax.dot_general(a, b, (((0,), (0,)), ((), ())), preferred_element_type=F32)


def place():
    near = lax.axis_size("ctx") // 4
    return lax.axis_index("ctx") // near, lax.axis_size("ctx") // near


def call(body, steps, ins, in_specs, out_shape, out_specs, cost, after=(), aliases=None, scratch=()):
    n_in, n_after = len(ins), len(after)

    def kernel(*refs):
        body(refs[:n_in], refs[n_in + n_after :])

    return pl.pallas_call(
        kernel,
        grid=(steps,),
        in_specs=list(in_specs) + [KEPT] * n_after,
        out_specs=list(out_specs),
        out_shape=list(out_shape),
        scratch_shapes=list(scratch),
        input_output_aliases=aliases or {},
        compiler_params=PARAMS,
        cost_estimate=pl.CostEstimate(
            flops=cost[0] // COST, bytes_accessed=cost[1] // COST, transcendentals=cost[2] // COST
        ),
    )(*ins, *after)


def first_pack(q, k, v, d, heads, hdim):
    rows = q.shape[0]

    def body(ins, rest):
        outs, held, arrive, leave = rest[:2], rest[2], rest[3], rest[4]
        z, ring = place()
        q, k, v, d = (ref.at[:, pl.ds(0, heads * hdim)] for ref in ins)

        def fetch(source, n):
            pltpu.make_async_copy(source, held.at[n], arrive.at[n]).start()

        for n, keys, queries in ((0, k, q), (1, v, d)):

            @pl.when(z == ring - 1)
            def _():
                fetch(queries, n)

            @pl.when(z != ring - 1)
            def _():
                fetch(keys, n)

            @pl.when(z == 0)
            def _():
                fetch(keys, 2 + n)

            @pl.when(z != 0)
            def _():
                fetch(queries, 2 + n)

        stores = []
        for n in range(4):
            pltpu.make_async_copy(q, held.at[n], arrive.at[n]).wait()
            store = pltpu.make_async_copy(held.at[n], outs[n // 2].at[n % 2], leave.at[n])
            store.start()
            stores.append(store)
        for store in stores:
            store.wait()

    shape = jax.ShapeDtypeStruct((2, rows, heads * hdim), BF16)
    return call(
        body,
        1,
        (q, k, v, d),
        [KEPT] * 4,
        [shape, shape],
        [KEPT] * 2,
        (0, 16 * rows * heads * hdim, 0),
        scratch=(
            pltpu.VMEM((4, rows, heads * hdim), BF16),
            pltpu.SemaphoreType.DMA((4,)),
            pltpu.SemaphoreType.DMA((4,)),
        ),
    )


def gate(packed, after):
    shapes = [jax.ShapeDtypeStruct(x.shape, x.dtype) for x in packed]

    def body(ins, outs):
        pass

    return call(
        body, 1, tuple(packed), [KEPT] * 2, shapes, [KEPT] * 2, (0, 0, 0), tuple(after), {0: 0, 1: 1}
    )


def row_stats(lse, output, d, after):
    heads, rows = lse.shape
    hdim = d.shape[1] // heads
    group = math.gcd(heads, 4)

    def body(ins, outs):
        lse_ref, o_ref, d_ref = ins
        (stats_ref,) = outs
        i = pl.program_id(0)
        ones = jnp.ones((8, hdim), BF16)

        @pl.when(i == 0)
        def _():
            stats_ref[0] = lse_ref[...]

        for g in range(group):
            cols = slice(g * hdim, (g + 1) * hdim)
            product = d_ref[:, cols].astype(F32) * o_ref[:, cols].astype(F32)
            high = product.astype(BF16)
            low = (product - high.astype(F32)).astype(BF16)
            delta = dot_nt(ones, high) + dot_nt(ones, low)
            stats_ref[1, pl.ds(i * group + g, 1), :] = delta[:1]

    block = pl.BlockSpec((rows, group * hdim), lambda i: (0, i))
    size = rows * heads * hdim
    (stats,) = call(
        body,
        heads // group,
        (lse, output, d),
        [pl.BlockSpec((heads, rows), lambda i: (0, 0)), block, block],
        [jax.ShapeDtypeStruct((2, heads, rows), F32)],
        [pl.BlockSpec((2, heads, rows), lambda i: (0, 0, 0))],
        (2 * size, 4 * size, 0),
        after,
    )
    return stats


def prob_terms(k, v, q, d, lse, delta, causal=False):
    scale = 1.0 / math.sqrt(q.shape[1])
    prob = jnp.exp2(dot_nt(k, q) * (scale * LOG2E) - lse * LOG2E)
    if causal:
        key_row = lax.broadcasted_iota(jnp.int32, prob.shape, 0)
        query_row = lax.broadcasted_iota(jnp.int32, prob.shape, 1)
        prob = jnp.where(key_row <= query_row, prob, 0.0)
    dscore = prob * (dot_nt(v, d) * scale - delta * scale)
    return prob.astype(BF16), dscore.astype(BF16)


def own_block(q, k, v, d, stats, first, heads, packed, after):
    rows = q.shape[0]
    hdim = q.shape[1] // stats.shape[1]
    group = math.gcd(first, heads, 4)
    cols = group * hdim

    def body(ins, outs):
        q_ref, k_ref, v_ref, d_ref, stats_ref = ins
        gq_ref, gk_ref, gv_ref = outs[:3]
        if packed:
            plus_ref, minus_ref = outs[3:]
            z, ring = place()

            def fill(ref, one, two):
                ref[0] = one[...]
                ref[1] = two[...]

            @pl.when(z == 0)
            def _():
                fill(plus_ref, k_ref, v_ref)
                fill(minus_ref, k_ref, v_ref)

            @pl.when((z != 0) & (z != ring - 1))
            def _():
                fill(plus_ref, k_ref, v_ref)
                fill(minus_ref, q_ref, d_ref)

            @pl.when(z == ring - 1)
            def _():
                fill(plus_ref, q_ref, d_ref)
                fill(minus_ref, q_ref, d_ref)

        for g in range(group):
            at = slice(g * hdim, (g + 1) * hdim)
            h = first + pl.program_id(0) * group + g
            qh, kh, vh, dh = q_ref[:, at], k_ref[:, at], v_ref[:, at], d_ref[:, at]
            lse = stats_ref[0, pl.ds(h, 1), :]
            delta = stats_ref[1, pl.ds(h, 1), :]
            prob, dscore = prob_terms(kh, vh, qh, dh, lse, delta, True)
            gq_ref[:, at] = dot_tn(dscore, kh)
            gk_ref[:, at] = dot_nn(dscore, qh)
            gv_ref[:, at] = dot_nn(prob, dh)

    block = pl.BlockSpec((rows, cols), lambda i: (0, first // group + i))
    out = pl.BlockSpec((rows, cols), lambda i: (0, i))
    sent = pl.BlockSpec((2, rows, cols), lambda i: (0, 0, i))
    shape = jax.ShapeDtypeStruct((rows, heads * hdim), F32)
    sent_shape = jax.ShapeDtypeStruct((2, rows, heads * hdim), BF16)
    size = rows * heads * hdim
    results = call(
        body,
        heads // group,
        (q, k, v, d, stats),
        [block] * 4 + [pl.BlockSpec(stats.shape, lambda i: (0, 0, 0))],
        [shape] * 3 + ([sent_shape] * 2 if packed else []),
        [out] * 3 + ([sent] * 2 if packed else []),
        (10 * rows * size, 28 * size, heads * rows * rows),
        after,
    )
    return results[:3], results[3:]


def chunk_grads(q, k, v, d, stats, plus, minus, pstats, mstats, own, outs, first, heads, after):
    rows, width = q.shape
    hdim = width // stats.shape[1]
    group = math.gcd(first, heads, 4)
    cols = group * hdim

    def body(ins, results):
        q_ref, k_ref, v_ref, d_ref, stats_ref, plus_ref, minus_ref, pstats_ref, mstats_ref = ins[:9]
        pq_ref, pk_ref, pv_ref = ins[9:12]
        gq_ref, gk_ref, gv_ref = results
        z, ring = place()

        def head(g):
            return slice(g * hdim, (g + 1) * hdim), first + pl.program_id(0) * group + g

        def keys_side(g, sent_ref, sent_stats):
            at, h = head(g)
            qh, dh = sent_ref[0, :, at], sent_ref[1, :, at]
            lse = sent_stats[0, pl.ds(h, 1), :]
            delta = sent_stats[1, pl.ds(h, 1), :]
            prob, dscore = prob_terms(k_ref[:, at], v_ref[:, at], qh, dh, lse, delta)
            return dot_nn(dscore, qh), dot_nn(prob, dh)

        def queries_side(g, sent_ref):
            at, h = head(g)
            kh, vh = sent_ref[0, :, at], sent_ref[1, :, at]
            lse = stats_ref[0, pl.ds(h, 1), :]
            delta = stats_ref[1, pl.ds(h, 1), :]
            _, dscore = prob_terms(kh, vh, q_ref[:, at], d_ref[:, at], lse, delta)
            return dot_tn(dscore, kh)

        @pl.when(z == 0)
        def _():
            for g in range(group):
                at, _ = head(g)
                upper_k, upper_v = keys_side(g, plus_ref, pstats_ref)
                lower_k, lower_v = keys_side(g, minus_ref, mstats_ref)
                gq_ref[:, at] = pq_ref[:, at].astype(BF16)
                gk_ref[:, at] = (pk_ref[:, at] + lower_k + upper_k).astype(BF16)
                gv_ref[:, at] = (pv_ref[:, at] + lower_v + upper_v).astype(BF16)

        @pl.when((z != 0) & (z != ring - 1))
        def _():
            for g in range(group):
                at, _ = head(g)
                lower_k, lower_v = keys_side(g, minus_ref, mstats_ref)
                gq_ref[:, at] = (pq_ref[:, at] + queries_side(g, plus_ref)).astype(BF16)
                gk_ref[:, at] = (pk_ref[:, at] + lower_k).astype(BF16)
                gv_ref[:, at] = (pv_ref[:, at] + lower_v).astype(BF16)

        @pl.when(z == ring - 1)
        def _():
            for g in range(group):
                at, _ = head(g)
                near = queries_side(g, plus_ref)
                far = queries_side(g, minus_ref)
                gq_ref[:, at] = (pq_ref[:, at] + near + far).astype(BF16)
                gk_ref[:, at] = pk_ref[:, at].astype(BF16)
                gv_ref[:, at] = pv_ref[:, at].astype(BF16)

    block = pl.BlockSpec((rows, cols), lambda i: (0, first // group + i))
    part = pl.BlockSpec((rows, cols), lambda i: (0, i))
    whole = pl.BlockSpec(stats.shape, lambda i: (0, 0, 0))
    sent = pl.BlockSpec((2, rows, cols), lambda i: (0, 0, i))
    size = rows * heads * hdim
    ins = (q, k, v, d, stats, plus, minus, pstats, mstats) + tuple(own)
    in_specs = [block] * 4 + [whole, sent, sent, whole, whole] + [part] * 3
    aliases = {}
    if outs is not None:
        aliases = {len(ins) + n: n for n in range(3)}
        ins += tuple(outs)
        in_specs += [KEPT] * 3
    return call(
        body,
        heads // group,
        ins,
        in_specs,
        [jax.ShapeDtypeStruct((rows, width), BF16)] * 3,
        [block] * 3,
        (16 * rows * size, 34 * size, 2 * heads * rows * rows),
        after,
        aliases,
    )


def per_device(query, key, value, output, grad_out, lse):
    heads = lse.shape[0]
    hdim = query.shape[1] // heads
    count = lax.axis_size("ctx")
    near = count // 4
    up = [(s, (s + near) % count) for s in range(count)]
    down = [(s, (s - near) % count) for s in range(count)]
    around = [(s, s + near - count) for s in range(count - near, count)]
    back = [(s, s - near) for s in range(near, count)]
    arrays = (query, key, value, grad_out)
    firsts = [sum(CHUNKS[:c]) for c in range(len(CHUNKS))]
    last = len(CHUNKS) - 1
    own, sent, plus, minus = {}, {}, {}, {}

    def prepare(c, packed, after):
        own[c], sent[c] = own_block(*arrays, stats, firsts[c], CHUNKS[c], packed, after)
        return own[c][:1]

    def send(c, after):
        if c > last:
            return ()
        if after:
            sent[c] = gate(sent[c], after)
        plus[c] = lax.ppermute(sent[c][0], "ctx", up)
        minus[c] = lax.ppermute(sent[c][1], "ctx", down)
        return sent[c][:1]

    first_sent = first_pack(*arrays, CHUNKS[0], hdim)
    sent[0] = first_sent
    send(0, ())
    stats = row_stats(lse, output, grad_out, first_sent[:1])
    pstats = lax.ppermute(stats, "ctx", around)
    mstats = lax.ppermute(stats, "ctx", back)
    prepare(1, True, ())
    token = send(1, (plus[0], minus[0]))
    token = prepare(2, True, token)
    token = send(2, (pstats, mstats, *token))
    token = prepare(0, False, token)
    sent[0] = first_sent
    outs = None
    for c in range(last + 1):
        outs = chunk_grads(
            *arrays, stats, plus[c], minus[c], pstats, mstats, own[c], outs, firsts[c], CHUNKS[c],
            token,
        )
        token = outs[:1]
        if c == 0:
            token = prepare(3, True, token)
        if c == 1:
            for later in range(4, last + 1):
                token = prepare(later, True, token)
        if c + 1 <= last and c + 3 <= last:
            token = send(c + 3, (plus[c + 1], minus[c + 1], *token))
        else:
            token = ()
    return tuple(outs)


def solution(mesh):
    in_specs = (
        P(("rep", "ctx"), None),
        P(("rep", "ctx"), None),
        P(("rep", "ctx"), None),
        P(("rep", "ctx"), None),
        P(("rep", "ctx"), None),
        P(None, ("rep", "ctx")),
    )
    out_specs = (P(("rep", "ctx"), None), P(("rep", "ctx"), None), P(("rep", "ctx"), None))
    return jax.shard_map(
        per_device, mesh=mesh, in_specs=in_specs, out_specs=out_specs, check_vma=False
    )
```

```python
import math

import jax
import jax.numpy as jnp
from jax import lax
from jax.experimental import pallas as pl
from jax.experimental.pallas import tpu as pltpu
from jax.sharding import PartitionSpec as P

F32 = jnp.float32
BF16 = jnp.bfloat16
VMEM_BYTES = 56 * 1024 * 1024
CHUNKS = (4, 4, 8, 8, 4, 2, 2)
OWN_VMEM = 30 << 20
CHUNK_VMEM = 24 << 20
COST = 100
LOG2E = math.log2(math.e)
KEPT = pl.BlockSpec(memory_space=pl.ANY)


def dot_nt(a, b):
    return lax.dot_general(a, b, (((1,), (1,)), ((), ())), preferred_element_type=F32)


def dot_nn(a, b):
    return lax.dot_general(a, b, (((1,), (0,)), ((), ())), preferred_element_type=F32)


def dot_tn(a, b):
    return lax.dot_general(a, b, (((0,), (0,)), ((), ())), preferred_element_type=F32)


def sides():
    index = lax.axis_index("ctx")
    near = lax.axis_size("ctx") // 4
    z = index // near
    top = lax.axis_size("ctx") // near - 1
    even = index % 2 == 0
    odd = index % 2 == 1
    sent_a = (even & (z == top)) | (odd & (z != 0))
    sent_b = (odd & (z == top)) | (even & (z != 0))
    come_a = (even & (z == 0)) | (odd & (z != top))
    come_b = (odd & (z == 0)) | (even & (z != top))
    return sent_a, sent_b, come_a, come_b


def fill(sent_a, sent_b, a_ref, b_ref, q, k, v, d):
    rows = q.shape[0]
    for flag, ref in ((sent_a, a_ref), (sent_b, b_ref)):

        @pl.when(flag)
        def _():
            ref[0, :rows] = q[...]
            ref[1, :rows] = d[...]

        @pl.when(jnp.logical_not(flag))
        def _():
            ref[0, :rows] = k[...]
            ref[1, :rows] = v[...]


def call(
    body, steps, ins, in_specs, out_shape, out_specs, cost, after=(), aliases=None, scratch=(),
    vmem=VMEM_BYTES,
):
    n_in, n_after = len(ins), len(after)

    def kernel(*refs):
        body(refs[:n_in], refs[n_in + n_after :])

    return pl.pallas_call(
        kernel,
        grid=(steps,),
        in_specs=list(in_specs) + [KEPT] * n_after,
        out_specs=list(out_specs),
        out_shape=list(out_shape),
        scratch_shapes=list(scratch),
        input_output_aliases=aliases or {},
        compiler_params=pltpu.CompilerParams(vmem_limit_bytes=vmem),
        cost_estimate=pl.CostEstimate(
            flops=cost[0] // COST, bytes_accessed=cost[1] // COST, transcendentals=cost[2] // COST
        ),
    )(*ins, *after)


def first_pack(q, k, v, d, heads, hdim):
    rows = q.shape[0]

    def body(ins, rest):
        outs, held, arrive, leave = rest[:2], rest[2], rest[3], rest[4]
        flags = sides()[:2]
        q, k, v, d = (ref.at[:, pl.ds(0, heads * hdim)] for ref in ins)

        def fetch(source, n):
            pltpu.make_async_copy(source, held.at[n], arrive.at[n]).start()

        for array, flag in enumerate(flags):
            for n, keys, queries in ((2 * array, k, q), (2 * array + 1, v, d)):

                @pl.when(flag)
                def _():
                    fetch(queries, n)

                @pl.when(jnp.logical_not(flag))
                def _():
                    fetch(keys, n)

        stores = []
        for n in range(4):
            pltpu.make_async_copy(q, held.at[n], arrive.at[n]).wait()
            store = pltpu.make_async_copy(held.at[n], outs[n // 2].at[n % 2], leave.at[n])
            store.start()
            stores.append(store)
        for store in stores:
            store.wait()

    shape = jax.ShapeDtypeStruct((2, rows, heads * hdim), BF16)
    return call(
        body,
        1,
        (q, k, v, d),
        [KEPT] * 4,
        [shape, shape],
        [KEPT] * 2,
        (0, 16 * rows * heads * hdim, 0),
        scratch=(
            pltpu.VMEM((4, rows, heads * hdim), BF16),
            pltpu.SemaphoreType.DMA((4,)),
            pltpu.SemaphoreType.DMA((4,)),
        ),
    )


def gate(packed, after):
    shapes = [jax.ShapeDtypeStruct(x.shape, x.dtype) for x in packed]

    def body(ins, outs):
        pass

    return call(
        body, 1, tuple(packed), [KEPT] * 2, shapes, [KEPT] * 2, (0, 0, 0), tuple(after), {0: 0, 1: 1},
        vmem=1 << 20,
    )


def row_stats(lse, output, d, after):
    heads, rows = lse.shape
    hdim = d.shape[1] // heads
    group = math.gcd(heads, 4)

    def body(ins, outs):
        lse_ref, o_ref, d_ref = ins
        (stats_ref,) = outs
        i = pl.program_id(0)
        ones = jnp.ones((8, hdim), BF16)

        @pl.when(i == 0)
        def _():
            stats_ref[0] = lse_ref[...]

        for g in range(group):
            cols = slice(g * hdim, (g + 1) * hdim)
            product = d_ref[:, cols].astype(F32) * o_ref[:, cols].astype(F32)
            high = product.astype(BF16)
            low = (product - high.astype(F32)).astype(BF16)
            delta = dot_nt(ones, high) + dot_nt(ones, low)
            stats_ref[1, pl.ds(i * group + g, 1), :] = delta[:1]

    block = pl.BlockSpec((rows, group * hdim), lambda i: (0, i))
    size = rows * heads * hdim
    (stats,) = call(
        body,
        heads // group,
        (lse, output, d),
        [pl.BlockSpec((heads, rows), lambda i: (0, 0)), block, block],
        [jax.ShapeDtypeStruct((2, heads, rows), F32)],
        [pl.BlockSpec((2, heads, rows), lambda i: (0, 0, 0))],
        (2 * size, 4 * size, 0),
        after,
    )
    return stats


def second_pack(q, k, v, d, stats, first, heads, hdim):
    rows = q.shape[0]
    cols = heads * hdim
    count = stats.shape[1]
    half = count // 2
    split = cols - rows

    def body(ins, outs):
        q_ref, k_ref, v_ref, d_ref, stats_ref = ins
        fill(*sides()[:2], *outs, q_ref, k_ref, v_ref, d_ref)
        for n in range(2):
            high = stats_ref[n].astype(BF16)
            low = (stats_ref[n] - high.astype(F32)).astype(BF16)
            for ref in outs:
                ref[n, rows : rows + count, :rows] = high
                ref[n, rows : rows + count, rows:] = low[:, :split]
                ref[n, rows + count :, : rows - split] = low[:half, split:]
                ref[n, rows + count :, rows - split :] = low[half:, split:]

    block = pl.BlockSpec((rows, cols), lambda i: (0, first // heads))
    shape = jax.ShapeDtypeStruct((2, rows + count + half, cols), BF16)
    size = rows * cols
    return call(
        body,
        1,
        (q, k, v, d, stats),
        [block] * 4 + [pl.BlockSpec(stats.shape, lambda i: (0, 0, 0))],
        [shape] * 2,
        [pl.BlockSpec(shape.shape, lambda i: (0, 0, 0))] * 2,
        (0, 16 * size, 0),
    )


def read_stats(come_a, come_b, stats):
    _, count, rows = stats.shape
    cols = come_a.shape[2]
    half = count // 2
    split = cols - rows

    def body(ins, outs):
        for sent, out in zip(ins, outs):
            for n in range(2):
                top = sent[n, :count, :].astype(F32)
                below = sent[n, count:, :].astype(F32)
                rest = jnp.concatenate([below[:, : rows - split], below[:, rows - split :]], axis=0)
                low = jnp.concatenate([top[:, rows:], rest], axis=1)
                out[n] = top[:, :rows] + low

    block = pl.BlockSpec((2, count + half, cols), lambda i: (0, rows // (count + half), 0))
    return call(
        body,
        1,
        (come_a, come_b),
        [block] * 2,
        [jax.ShapeDtypeStruct(stats.shape, F32)] * 2,
        [pl.BlockSpec(stats.shape, lambda i: (0, 0, 0))] * 2,
        (0, 4 * count * rows, 0),
        vmem=4 << 20,
    )


def prob_terms(k, v, q, d, lse, delta, causal=False):
    scale = 1.0 / math.sqrt(q.shape[1])
    prob = jnp.exp2(dot_nt(k, q) * (scale * LOG2E) - lse * LOG2E)
    if causal:
        key_row = lax.broadcasted_iota(jnp.int32, prob.shape, 0)
        query_row = lax.broadcasted_iota(jnp.int32, prob.shape, 1)
        prob = jnp.where(key_row <= query_row, prob, 0.0)
    dscore = prob * (dot_nt(v, d) * scale - delta * scale)
    return prob.astype(BF16), dscore.astype(BF16)


def own_block(q, k, v, d, stats, first, heads, packed, after):
    rows = q.shape[0]
    hdim = q.shape[1] // stats.shape[1]
    group = math.gcd(first, heads, 4)
    cols = group * hdim

    def body(ins, outs):
        q_ref, k_ref, v_ref, d_ref, stats_ref = ins
        gq_ref, gk_ref, gv_ref = outs[:3]
        if packed:
            fill(*sides()[:2], *outs[3:], q_ref, k_ref, v_ref, d_ref)
        for g in range(group):
            at = slice(g * hdim, (g + 1) * hdim)
            h = first + pl.program_id(0) * group + g
            qh, kh, vh, dh = q_ref[:, at], k_ref[:, at], v_ref[:, at], d_ref[:, at]
            lse = stats_ref[0, pl.ds(h, 1), :]
            delta = stats_ref[1, pl.ds(h, 1), :]
            prob, dscore = prob_terms(kh, vh, qh, dh, lse, delta, True)
            gq_ref[:, at] = dot_tn(dscore, kh)
            gk_ref[:, at] = dot_nn(dscore, qh)
            gv_ref[:, at] = dot_nn(prob, dh)

    block = pl.BlockSpec((rows, cols), lambda i: (0, first // group + i))
    out = pl.BlockSpec((rows, cols), lambda i: (0, i))
    sent = pl.BlockSpec((2, rows, cols), lambda i: (0, 0, i))
    shape = jax.ShapeDtypeStruct((rows, heads * hdim), F32)
    sent_shape = jax.ShapeDtypeStruct((2, rows, heads * hdim), BF16)
    size = rows * heads * hdim
    results = call(
        body,
        heads // group,
        (q, k, v, d, stats),
        [block] * 4 + [pl.BlockSpec(stats.shape, lambda i: (0, 0, 0))],
        [shape] * 3 + ([sent_shape] * 2 if packed else []),
        [out] * 3 + ([sent] * 2 if packed else []),
        (10 * rows * size, 28 * size, heads * rows * rows),
        after,
        vmem=OWN_VMEM,
    )
    return results[:3], results[3:]


def chunk_grads(q, k, v, d, stats, come_a, come_b, astats, bstats, own, outs, first, heads, after):
    rows, width = q.shape
    hdim = width // stats.shape[1]
    group = math.gcd(first, heads, 4)
    cols = group * hdim

    def body(ins, results):
        q_ref, k_ref, v_ref, d_ref, stats_ref, a_ref, b_ref, astats_ref, bstats_ref = ins[:9]
        pq_ref, pk_ref, pv_ref = ins[9:12]
        gq_ref, gk_ref, gv_ref = results
        _, _, come_a, come_b = sides()

        def head(g):
            return slice(g * hdim, (g + 1) * hdim), first + pl.program_id(0) * group + g

        def keys_side(g, sent_ref, sent_stats):
            at, h = head(g)
            qh, dh = sent_ref[0, :, at], sent_ref[1, :, at]
            lse = sent_stats[0, pl.ds(h, 1), :]
            delta = sent_stats[1, pl.ds(h, 1), :]
            prob, dscore = prob_terms(k_ref[:, at], v_ref[:, at], qh, dh, lse, delta)
            return dot_nn(dscore, qh), dot_nn(prob, dh)

        def queries_side(g, sent_ref):
            at, h = head(g)
            kh, vh = sent_ref[0, :, at], sent_ref[1, :, at]
            lse = stats_ref[0, pl.ds(h, 1), :]
            delta = stats_ref[1, pl.ds(h, 1), :]
            _, dscore = prob_terms(kh, vh, q_ref[:, at], d_ref[:, at], lse, delta)
            return dot_tn(dscore, kh)

        def keys_only():
            for g in range(group):
                at, _ = head(g)
                one_k, one_v = keys_side(g, a_ref, astats_ref)
                two_k, two_v = keys_side(g, b_ref, bstats_ref)
                gq_ref[:, at] = pq_ref[:, at].astype(BF16)
                gk_ref[:, at] = (pk_ref[:, at] + one_k + two_k).astype(BF16)
                gv_ref[:, at] = (pv_ref[:, at] + one_v + two_v).astype(BF16)

        def both(q_ref, q_stats, k_ref):
            for g in range(group):
                at, _ = head(g)
                one_k, one_v = keys_side(g, q_ref, q_stats)
                gq_ref[:, at] = (pq_ref[:, at] + queries_side(g, k_ref)).astype(BF16)
                gk_ref[:, at] = (pk_ref[:, at] + one_k).astype(BF16)
                gv_ref[:, at] = (pv_ref[:, at] + one_v).astype(BF16)

        def queries_only():
            for g in range(group):
                at, _ = head(g)
                one = queries_side(g, a_ref)
                two = queries_side(g, b_ref)
                gq_ref[:, at] = (pq_ref[:, at] + one + two).astype(BF16)
                gk_ref[:, at] = pk_ref[:, at].astype(BF16)
                gv_ref[:, at] = pv_ref[:, at].astype(BF16)

        no_a, no_b = jnp.logical_not(come_a), jnp.logical_not(come_b)
        pl.when(come_a & come_b)(keys_only)
        pl.when(come_a & no_b)(lambda: both(a_ref, astats_ref, b_ref))
        pl.when(no_a & come_b)(lambda: both(b_ref, bstats_ref, a_ref))
        pl.when(no_a & no_b)(queries_only)

    block = pl.BlockSpec((rows, cols), lambda i: (0, first // group + i))
    part = pl.BlockSpec((rows, cols), lambda i: (0, i))
    whole = pl.BlockSpec(stats.shape, lambda i: (0, 0, 0))
    sent = pl.BlockSpec((2, rows, cols), lambda i: (0, 0, i))
    size = rows * heads * hdim
    ins = (q, k, v, d, stats, come_a, come_b, astats, bstats) + tuple(own)
    in_specs = [block] * 4 + [whole, sent, sent, whole, whole] + [part] * 3
    aliases = {}
    if outs is not None:
        aliases = {len(ins) + n: n for n in range(3)}
        ins += tuple(outs)
        in_specs += [KEPT] * 3
    return call(
        body,
        heads // group,
        ins,
        in_specs,
        [jax.ShapeDtypeStruct((rows, width), BF16)] * 3,
        [block] * 3,
        (16 * rows * size, 34 * size, 2 * heads * rows * rows),
        after,
        aliases,
        vmem=CHUNK_VMEM,
    )


def per_device(query, key, value, output, grad_out, lse):
    heads = lse.shape[0]
    hdim = query.shape[1] // heads
    count = lax.axis_size("ctx")
    near = count // 4
    way_a = [(s, (s + (near if s % 2 == 0 else -near)) % count) for s in range(count)]
    way_b = [(s, (s + (-near if s % 2 == 0 else near)) % count) for s in range(count)]
    arrays = (query, key, value, grad_out)
    firsts = [sum(CHUNKS[:c]) for c in range(len(CHUNKS))]
    last = len(CHUNKS) - 1
    own, sent, come_a, come_b = {}, {}, {}, {}

    def prepare(c, packed, after):
        own[c], sent[c] = own_block(*arrays, stats, firsts[c], CHUNKS[c], packed, after)
        return own[c][:1]

    def send(c, after):
        if c > last:
            return ()
        if after:
            sent[c] = gate(sent[c], after)
        come_a[c] = lax.ppermute(sent[c][0], "ctx", way_a)
        come_b[c] = lax.ppermute(sent[c][1], "ctx", way_b)
        return sent[c][:1]

    first_sent = first_pack(*arrays, CHUNKS[0], hdim)
    sent[0] = first_sent
    send(0, ())
    stats = row_stats(lse, output, grad_out, first_sent[:1])
    second_sent = second_pack(*arrays, stats, firsts[1], CHUNKS[1], hdim)
    sent[1] = second_sent
    send(1, ())
    token = prepare(2, True, second_sent[:1])
    token = send(2, (come_a[0], come_b[0], *token))
    token = prepare(0, False, token)
    token = prepare(1, False, token)
    for c in range(3, last + 1):
        token = prepare(c, True, token)
    astats, bstats = read_stats(come_a[1], come_b[1], stats)
    token = send(3, (astats, *token))
    outs = None
    for c in range(last + 1):
        if c > 1:
            token = send(c + 2, (come_a[c], come_b[c], *outs[:1]))
        outs = chunk_grads(
            *arrays, stats, come_a[c], come_b[c], astats, bstats, own[c], outs, firsts[c], CHUNKS[c],
            token,
        )
        token = ()
    return tuple(outs)


def solution(mesh):
    in_specs = (
        P(("rep", "ctx"), None),
        P(("rep", "ctx"), None),
        P(("rep", "ctx"), None),
        P(("rep", "ctx"), None),
        P(("rep", "ctx"), None),
        P(None, ("rep", "ctx")),
    )
    out_specs = (P(("rep", "ctx"), None), P(("rep", "ctx"), None), P(("rep", "ctx"), None))
    return jax.shard_map(
        per_device, mesh=mesh, in_specs=in_specs, out_specs=out_specs, check_vma=False
    )
```

```python
import math

import jax
import jax.numpy as jnp
from jax import lax
from jax.experimental import pallas as pl
from jax.experimental.pallas import tpu as pltpu
from jax.sharding import PartitionSpec as P

F32 = jnp.float32
BF16 = jnp.bfloat16
VMEM_BYTES = 56 * 1024 * 1024
CHUNKS = (4, 4, 8, 8, 4, 2, 2)
OWN_VMEM = 30 << 20
CHUNK_VMEM = 24 << 20
COST = 100
LOG2E = math.log2(math.e)
KEPT = pl.BlockSpec(memory_space=pl.ANY)
TOKEN = jax.ShapeDtypeStruct((8, 128), F32)
TOKEN_SPEC = pl.BlockSpec((8, 128), lambda i: (0, 0))


def dot_nt(a, b):
    return lax.dot_general(a, b, (((1,), (1,)), ((), ())), preferred_element_type=F32)


def dot_nn(a, b):
    return lax.dot_general(a, b, (((1,), (0,)), ((), ())), preferred_element_type=F32)


def dot_tn(a, b):
    return lax.dot_general(a, b, (((0,), (0,)), ((), ())), preferred_element_type=F32)


def sides():
    index = lax.axis_index("ctx")
    near = lax.axis_size("ctx") // 4
    z = index // near
    top = lax.axis_size("ctx") // near - 1
    even = index % 2 == 0
    odd = index % 2 == 1
    sent_a = (even & (z == top)) | (odd & (z != 0))
    sent_b = (odd & (z == top)) | (even & (z != 0))
    come_a = (even & (z == 0)) | (odd & (z != top))
    come_b = (odd & (z == 0)) | (even & (z != top))
    return sent_a, sent_b, come_a, come_b


def fill(sent_a, sent_b, a_ref, b_ref, q, k, v, d):
    rows = q.shape[0]
    for flag, ref in ((sent_a, a_ref), (sent_b, b_ref)):

        @pl.when(flag)
        def _():
            ref[0, :rows] = q[...]
            ref[1, :rows] = d[...]

        @pl.when(jnp.logical_not(flag))
        def _():
            ref[0, :rows] = k[...]
            ref[1, :rows] = v[...]


def call(
    body, steps, ins, in_specs, out_shape, out_specs, cost, after=(), aliases=None, scratch=(),
    vmem=VMEM_BYTES,
):
    n_in, n_after = len(ins), len(after)

    def kernel(*refs):
        body(refs[:n_in], refs[n_in + n_after :])

    return pl.pallas_call(
        kernel,
        grid=(steps,),
        in_specs=list(in_specs) + [KEPT] * n_after,
        out_specs=list(out_specs),
        out_shape=list(out_shape),
        scratch_shapes=list(scratch),
        input_output_aliases=aliases or {},
        compiler_params=pltpu.CompilerParams(vmem_limit_bytes=vmem),
        cost_estimate=pl.CostEstimate(
            flops=cost[0] // COST, bytes_accessed=cost[1] // COST, transcendentals=cost[2] // COST
        ),
    )(*ins, *after)


def first_pack(q, k, v, d, heads, hdim):
    rows = q.shape[0]

    def body(ins, rest):
        outs, held, arrive, leave = rest[:2], rest[2], rest[3], rest[4]
        flags = sides()[:2]
        q, k, v, d = (ref.at[:, pl.ds(0, heads * hdim)] for ref in ins)

        def fetch(source, n):
            pltpu.make_async_copy(source, held.at[n], arrive.at[n]).start()

        for array, flag in enumerate(flags):
            for n, keys, queries in ((2 * array, k, q), (2 * array + 1, v, d)):

                @pl.when(flag)
                def _():
                    fetch(queries, n)

                @pl.when(jnp.logical_not(flag))
                def _():
                    fetch(keys, n)

        stores = []
        for n in range(4):
            pltpu.make_async_copy(q, held.at[n], arrive.at[n]).wait()
            store = pltpu.make_async_copy(held.at[n], outs[n // 2].at[n % 2], leave.at[n])
            store.start()
            stores.append(store)
        for store in stores:
            store.wait()

    shape = jax.ShapeDtypeStruct((2, rows, heads * hdim), BF16)
    return call(
        body,
        1,
        (q, k, v, d),
        [KEPT] * 4,
        [shape, shape],
        [KEPT] * 2,
        (0, 16 * rows * heads * hdim, 0),
        scratch=(
            pltpu.VMEM((4, rows, heads * hdim), BF16),
            pltpu.SemaphoreType.DMA((4,)),
            pltpu.SemaphoreType.DMA((4,)),
        ),
    )


def gate(packed, after):
    shapes = [jax.ShapeDtypeStruct(x.shape, x.dtype) for x in packed]

    def body(ins, outs):
        outs[2][...] = jnp.zeros_like(outs[2])

    results = call(
        body,
        1,
        tuple(packed),
        [KEPT] * 2,
        shapes + [TOKEN],
        [KEPT] * 2 + [TOKEN_SPEC],
        (0, 0, 0),
        tuple(after),
        {0: 0, 1: 1},
        vmem=1 << 20,
    )
    return results[:2], results[2:]


def row_stats(lse, output, d, after):
    heads, rows = lse.shape
    hdim = d.shape[1] // heads
    group = math.gcd(heads, 4)

    def body(ins, outs):
        lse_ref, o_ref, d_ref = ins
        (stats_ref,) = outs
        i = pl.program_id(0)
        ones = jnp.ones((8, hdim), BF16)

        @pl.when(i == 0)
        def _():
            stats_ref[0] = lse_ref[...]

        for g in range(group):
            cols = slice(g * hdim, (g + 1) * hdim)
            product = d_ref[:, cols].astype(F32) * o_ref[:, cols].astype(F32)
            high = product.astype(BF16)
            low = (product - high.astype(F32)).astype(BF16)
            delta = dot_nt(ones, high) + dot_nt(ones, low)
            stats_ref[1, pl.ds(i * group + g, 1), :] = delta[:1]

    block = pl.BlockSpec((rows, group * hdim), lambda i: (0, i))
    size = rows * heads * hdim
    (stats,) = call(
        body,
        heads // group,
        (lse, output, d),
        [pl.BlockSpec((heads, rows), lambda i: (0, 0)), block, block],
        [jax.ShapeDtypeStruct((2, heads, rows), F32)],
        [pl.BlockSpec((2, heads, rows), lambda i: (0, 0, 0))],
        (2 * size, 4 * size, 0),
        after,
    )
    return stats


def second_pack(q, k, v, d, stats, first, heads, hdim):
    rows = q.shape[0]
    cols = heads * hdim
    count = stats.shape[1]
    half = count // 2
    split = cols - rows

    def body(ins, outs):
        q_ref, k_ref, v_ref, d_ref, stats_ref = ins
        fill(*sides()[:2], *outs, q_ref, k_ref, v_ref, d_ref)
        for n in range(2):
            high = stats_ref[n].astype(BF16)
            low = (stats_ref[n] - high.astype(F32)).astype(BF16)
            for ref in outs:
                ref[n, rows : rows + count, :rows] = high
                ref[n, rows : rows + count, rows:] = low[:, :split]
                ref[n, rows + count :, : rows - split] = low[:half, split:]
                ref[n, rows + count :, rows - split :] = low[half:, split:]

    block = pl.BlockSpec((rows, cols), lambda i: (0, first // heads))
    shape = jax.ShapeDtypeStruct((2, rows + count + half, cols), BF16)
    size = rows * cols
    return call(
        body,
        1,
        (q, k, v, d, stats),
        [block] * 4 + [pl.BlockSpec(stats.shape, lambda i: (0, 0, 0))],
        [shape] * 2,
        [pl.BlockSpec(shape.shape, lambda i: (0, 0, 0))] * 2,
        (0, 16 * size, 0),
    )


def read_stats(come_a, come_b, stats):
    _, count, rows = stats.shape
    cols = come_a.shape[2]
    half = count // 2
    split = cols - rows

    def body(ins, outs):
        for sent, out in zip(ins, outs):
            for n in range(2):
                top = sent[n, :count, :].astype(F32)
                below = sent[n, count:, :].astype(F32)
                rest = jnp.concatenate([below[:, : rows - split], below[:, rows - split :]], axis=0)
                low = jnp.concatenate([top[:, rows:], rest], axis=1)
                out[n] = top[:, :rows] + low

    block = pl.BlockSpec((2, count + half, cols), lambda i: (0, rows // (count + half), 0))
    return call(
        body,
        1,
        (come_a, come_b),
        [block] * 2,
        [jax.ShapeDtypeStruct(stats.shape, F32)] * 2,
        [pl.BlockSpec(stats.shape, lambda i: (0, 0, 0))] * 2,
        (0, 4 * count * rows, 0),
        vmem=4 << 20,
    )


def prob_terms(k, v, q, d, lse, delta, causal=False):
    scale = 1.0 / math.sqrt(q.shape[1])
    prob = jnp.exp2(dot_nt(k, q) * (scale * LOG2E) - lse * LOG2E)
    if causal:
        key_row = lax.broadcasted_iota(jnp.int32, prob.shape, 0)
        query_row = lax.broadcasted_iota(jnp.int32, prob.shape, 1)
        prob = jnp.where(key_row <= query_row, prob, 0.0)
    dscore = prob * (dot_nt(v, d) * scale - delta * scale)
    return prob.astype(BF16), dscore.astype(BF16)


def own_block(q, k, v, d, stats, first, heads, packed, after):
    rows = q.shape[0]
    hdim = q.shape[1] // stats.shape[1]
    group = math.gcd(first, heads, 4)
    cols = group * hdim

    def body(ins, outs):
        q_ref, k_ref, v_ref, d_ref, stats_ref = ins
        gq_ref, gk_ref, gv_ref, token_ref = outs[:4]
        token_ref[...] = jnp.zeros_like(token_ref)
        if packed:
            fill(*sides()[:2], *outs[4:], q_ref, k_ref, v_ref, d_ref)
        for g in range(group):
            at = slice(g * hdim, (g + 1) * hdim)
            h = first + pl.program_id(0) * group + g
            qh, kh, vh, dh = q_ref[:, at], k_ref[:, at], v_ref[:, at], d_ref[:, at]
            lse = stats_ref[0, pl.ds(h, 1), :]
            delta = stats_ref[1, pl.ds(h, 1), :]
            prob, dscore = prob_terms(kh, vh, qh, dh, lse, delta, True)
            gq_ref[:, at] = dot_tn(dscore, kh)
            gk_ref[:, at] = dot_nn(dscore, qh)
            gv_ref[:, at] = dot_nn(prob, dh)

    block = pl.BlockSpec((rows, cols), lambda i: (0, first // group + i))
    out = pl.BlockSpec((rows, cols), lambda i: (0, i))
    sent = pl.BlockSpec((2, rows, cols), lambda i: (0, 0, i))
    shape = jax.ShapeDtypeStruct((rows, heads * hdim), F32)
    sent_shape = jax.ShapeDtypeStruct((2, rows, heads * hdim), BF16)
    size = rows * heads * hdim
    results = call(
        body,
        heads // group,
        (q, k, v, d, stats),
        [block] * 4 + [pl.BlockSpec(stats.shape, lambda i: (0, 0, 0))],
        [shape] * 3 + [TOKEN] + ([sent_shape] * 2 if packed else []),
        [out] * 3 + [TOKEN_SPEC] + ([sent] * 2 if packed else []),
        (10 * rows * size, 28 * size, heads * rows * rows),
        after,
        vmem=OWN_VMEM,
    )
    return results[:3], results[3:4], results[4:]


def chunk_grads(q, k, v, d, stats, come_a, come_b, astats, bstats, own, outs, first, heads, after):
    rows, width = q.shape
    hdim = width // stats.shape[1]
    group = math.gcd(first, heads, 4)
    cols = group * hdim

    def body(ins, results):
        q_ref, k_ref, v_ref, d_ref, stats_ref, a_ref, b_ref, astats_ref, bstats_ref = ins[:9]
        pq_ref, pk_ref, pv_ref = ins[9:12]
        gq_ref, gk_ref, gv_ref, token_ref = results
        token_ref[...] = jnp.zeros_like(token_ref)
        _, _, come_a, come_b = sides()

        def head(g):
            return slice(g * hdim, (g + 1) * hdim), first + pl.program_id(0) * group + g

        def keys_side(g, sent_ref, sent_stats):
            at, h = head(g)
            qh, dh = sent_ref[0, :, at], sent_ref[1, :, at]
            lse = sent_stats[0, pl.ds(h, 1), :]
            delta = sent_stats[1, pl.ds(h, 1), :]
            prob, dscore = prob_terms(k_ref[:, at], v_ref[:, at], qh, dh, lse, delta)
            return dot_nn(dscore, qh), dot_nn(prob, dh)

        def queries_side(g, sent_ref):
            at, h = head(g)
            kh, vh = sent_ref[0, :, at], sent_ref[1, :, at]
            lse = stats_ref[0, pl.ds(h, 1), :]
            delta = stats_ref[1, pl.ds(h, 1), :]
            _, dscore = prob_terms(kh, vh, q_ref[:, at], d_ref[:, at], lse, delta)
            return dot_tn(dscore, kh)

        def joined(part, at):
            return jnp.concatenate([a_ref[part, :, at], b_ref[part, :, at]], axis=0)

        def keys_only():
            for g in range(group):
                at, h = head(g)
                qh, dh = joined(0, at), joined(1, at)
                lse, delta = (
                    jnp.concatenate(
                        [astats_ref[n, pl.ds(h, 1), :], bstats_ref[n, pl.ds(h, 1), :]], axis=1
                    )
                    for n in range(2)
                )
                prob, dscore = prob_terms(k_ref[:, at], v_ref[:, at], qh, dh, lse, delta)
                gq_ref[:, at] = pq_ref[:, at].astype(BF16)
                gk_ref[:, at] = (pk_ref[:, at] + dot_nn(dscore, qh)).astype(BF16)
                gv_ref[:, at] = (pv_ref[:, at] + dot_nn(prob, dh)).astype(BF16)

        def both(q_ref, q_stats, k_ref):
            for g in range(group):
                at, _ = head(g)
                one_k, one_v = keys_side(g, q_ref, q_stats)
                gq_ref[:, at] = (pq_ref[:, at] + queries_side(g, k_ref)).astype(BF16)
                gk_ref[:, at] = (pk_ref[:, at] + one_k).astype(BF16)
                gv_ref[:, at] = (pv_ref[:, at] + one_v).astype(BF16)

        def queries_only():
            for g in range(group):
                at, h = head(g)
                kh, vh = joined(0, at), joined(1, at)
                lse = stats_ref[0, pl.ds(h, 1), :]
                delta = stats_ref[1, pl.ds(h, 1), :]
                _, dscore = prob_terms(kh, vh, q_ref[:, at], d_ref[:, at], lse, delta)
                gq_ref[:, at] = (pq_ref[:, at] + dot_tn(dscore, kh)).astype(BF16)
                gk_ref[:, at] = pk_ref[:, at].astype(BF16)
                gv_ref[:, at] = pv_ref[:, at].astype(BF16)

        no_a, no_b = jnp.logical_not(come_a), jnp.logical_not(come_b)
        pl.when(come_a & come_b)(keys_only)
        pl.when(come_a & no_b)(lambda: both(a_ref, astats_ref, b_ref))
        pl.when(no_a & come_b)(lambda: both(b_ref, bstats_ref, a_ref))
        pl.when(no_a & no_b)(queries_only)

    block = pl.BlockSpec((rows, cols), lambda i: (0, first // group + i))
    part = pl.BlockSpec((rows, cols), lambda i: (0, i))
    whole = pl.BlockSpec(stats.shape, lambda i: (0, 0, 0))
    sent = pl.BlockSpec((2, rows, cols), lambda i: (0, 0, i))
    size = rows * heads * hdim
    ins = (q, k, v, d, stats, come_a, come_b, astats, bstats) + tuple(own)
    in_specs = [block] * 4 + [whole, sent, sent, whole, whole] + [part] * 3
    aliases = {}
    if outs is not None:
        aliases = {len(ins) + n: n for n in range(3)}
        ins += tuple(outs)
        in_specs += [KEPT] * 3
    results = call(
        body,
        heads // group,
        ins,
        in_specs,
        [jax.ShapeDtypeStruct((rows, width), BF16)] * 3 + [TOKEN],
        [block] * 3 + [TOKEN_SPEC],
        (16 * rows * size, 34 * size, 2 * heads * rows * rows),
        after,
        aliases,
        vmem=CHUNK_VMEM,
    )
    return results[:3], results[3:]


def per_device(query, key, value, output, grad_out, lse):
    heads = lse.shape[0]
    hdim = query.shape[1] // heads
    count = lax.axis_size("ctx")
    near = count // 4
    way_a = [(s, (s + (near if s % 2 == 0 else -near)) % count) for s in range(count)]
    way_b = [(s, (s + (-near if s % 2 == 0 else near)) % count) for s in range(count)]
    arrays = (query, key, value, grad_out)
    firsts = [sum(CHUNKS[:c]) for c in range(len(CHUNKS))]
    last = len(CHUNKS) - 1
    own, sent, come_a, come_b = {}, {}, {}, {}

    def prepare(c, packed, after):
        own[c], token, packs = own_block(*arrays, stats, firsts[c], CHUNKS[c], packed, after)
        if packed:
            sent[c] = packs
        return token

    def send(c, after):
        if c > last:
            return ()
        token = ()
        if after:
            sent[c], token = gate(sent[c], after)
        come_a[c] = lax.ppermute(sent[c][0], "ctx", way_a)
        come_b[c] = lax.ppermute(sent[c][1], "ctx", way_b)
        return token

    sent[0] = first_pack(*arrays, CHUNKS[0], hdim)
    send(0, ())
    stats = row_stats(lse, output, grad_out, sent[0][:1])
    second_sent = second_pack(*arrays, stats, firsts[1], CHUNKS[1], hdim)
    sent[1] = second_sent
    send(1, ())
    token = prepare(2, True, second_sent[:1])
    token = send(2, (come_a[0], come_b[0], *token))
    token = prepare(0, False, token)
    token = prepare(1, False, token)
    for c in range(3, last + 1):
        token = prepare(c, True, token)
    astats, bstats = read_stats(come_a[1], come_b[1], stats)
    token = send(3, (astats, *token))
    outs, done = None, ()
    for c in range(last + 1):
        if c > 1:
            token = send(c + 2, (come_a[c], come_b[c], *done))
        outs, done = chunk_grads(
            *arrays, stats, come_a[c], come_b[c], astats, bstats, own[c], outs, firsts[c],
            CHUNKS[c], token,
        )
        token = ()
    return tuple(outs)


def solution(mesh):
    in_specs = (
        P(("rep", "ctx"), None),
        P(("rep", "ctx"), None),
        P(("rep", "ctx"), None),
        P(("rep", "ctx"), None),
        P(("rep", "ctx"), None),
        P(None, ("rep", "ctx")),
    )
    out_specs = (P(("rep", "ctx"), None), P(("rep", "ctx"), None), P(("rep", "ctx"), None))
    return jax.shard_map(
        per_device, mesh=mesh, in_specs=in_specs, out_specs=out_specs, check_vma=False
    )
```

```python
import math

import jax
import jax.numpy as jnp
from jax import lax
from jax.experimental import pallas as pl
from jax.experimental.pallas import tpu as pltpu
from jax.sharding import PartitionSpec as P

F32 = jnp.float32
BF16 = jnp.bfloat16
VMEM_BYTES = 56 * 1024 * 1024
CHUNKS = (4, 4, 8, 8, 4, 2, 2)
OWN_VMEM = 30 << 20
CHUNK_VMEM = 24 << 20
COST = 100
ROWS = 8
LOG2E = math.log2(math.e)
KEPT = pl.BlockSpec(memory_space=pl.ANY)
TOKEN = jax.ShapeDtypeStruct((8, 128), F32)
TOKEN_SPEC = pl.BlockSpec((8, 128), lambda i: (0, 0))


def dot_nt(a, b):
    return lax.dot_general(a, b, (((1,), (1,)), ((), ())), preferred_element_type=F32)


def dot_nn(a, b):
    return lax.dot_general(a, b, (((1,), (0,)), ((), ())), preferred_element_type=F32)


def dot_tn(a, b):
    return lax.dot_general(a, b, (((0,), (0,)), ((), ())), preferred_element_type=F32)


def sides():
    index = lax.axis_index("ctx")
    near = lax.axis_size("ctx") // 4
    z = index // near
    top = lax.axis_size("ctx") // near - 1
    even = index % 2 == 0
    odd = index % 2 == 1
    sent_a = (even & (z == top)) | (odd & (z != 0))
    sent_b = (odd & (z == top)) | (even & (z != 0))
    come_a = (even & (z == 0)) | (odd & (z != top))
    come_b = (odd & (z == 0)) | (even & (z != top))
    return sent_a, sent_b, come_a, come_b


def fill(sent_a, sent_b, a_ref, b_ref, q, k, v, d):
    rows = q.shape[0]
    for flag, ref in ((sent_a, a_ref), (sent_b, b_ref)):

        @pl.when(flag)
        def _():
            ref[0, :rows] = q[...]
            ref[1, :rows] = d[...]

        @pl.when(jnp.logical_not(flag))
        def _():
            ref[0, :rows] = k[...]
            ref[1, :rows] = v[...]


def call(
    body, steps, ins, in_specs, out_shape, out_specs, cost, after=(), aliases=None, scratch=(),
    vmem=VMEM_BYTES,
):
    n_in, n_after = len(ins), len(after)

    def kernel(*refs):
        body(refs[:n_in], refs[n_in + n_after :])

    return pl.pallas_call(
        kernel,
        grid=(steps,),
        in_specs=list(in_specs) + [KEPT] * n_after,
        out_specs=list(out_specs),
        out_shape=list(out_shape),
        scratch_shapes=list(scratch),
        input_output_aliases=aliases or {},
        compiler_params=pltpu.CompilerParams(vmem_limit_bytes=vmem),
        cost_estimate=pl.CostEstimate(
            flops=cost[0] // COST, bytes_accessed=cost[1] // COST, transcendentals=cost[2] // COST
        ),
    )(*ins, *after)


def first_pack(q, k, v, d, heads, hdim):
    rows = q.shape[0]

    def body(ins, rest):
        outs, held, arrive, leave = rest[:2], rest[2], rest[3], rest[4]
        flags = sides()[:2]
        q, k, v, d = (ref.at[:, pl.ds(0, heads * hdim)] for ref in ins)

        def fetch(source, n):
            pltpu.make_async_copy(source, held.at[n], arrive.at[n]).start()

        for array, flag in enumerate(flags):
            for n, keys, queries in ((2 * array, k, q), (2 * array + 1, v, d)):

                @pl.when(flag)
                def _():
                    fetch(queries, n)

                @pl.when(jnp.logical_not(flag))
                def _():
                    fetch(keys, n)

        stores = []
        for n in range(4):
            pltpu.make_async_copy(q, held.at[n], arrive.at[n]).wait()
            store = pltpu.make_async_copy(held.at[n], outs[n // 2].at[n % 2], leave.at[n])
            store.start()
            stores.append(store)
        for store in stores:
            store.wait()

    shape = jax.ShapeDtypeStruct((2, rows, heads * hdim), BF16)
    return call(
        body,
        1,
        (q, k, v, d),
        [KEPT] * 4,
        [shape, shape],
        [KEPT] * 2,
        (0, 16 * rows * heads * hdim, 0),
        scratch=(
            pltpu.VMEM((4, rows, heads * hdim), BF16),
            pltpu.SemaphoreType.DMA((4,)),
            pltpu.SemaphoreType.DMA((4,)),
        ),
    )


def gate(packed, after):
    shapes = [jax.ShapeDtypeStruct(x.shape, x.dtype) for x in packed]

    def body(ins, outs):
        outs[2][...] = jnp.zeros_like(outs[2])

    results = call(
        body,
        1,
        tuple(packed),
        [KEPT] * 2,
        shapes + [TOKEN],
        [KEPT] * 2 + [TOKEN_SPEC],
        (0, 0, 0),
        tuple(after),
        {0: 0, 1: 1},
        vmem=1 << 20,
    )
    return results[:2], results[2:]


def row_stats(lse, output, d, after):
    heads, rows = lse.shape
    hdim = d.shape[1] // heads
    group = math.gcd(heads, 4)

    def body(ins, outs):
        lse_ref, o_ref, d_ref = ins
        (stats_ref,) = outs
        i = pl.program_id(0)
        ones = jnp.ones((8, hdim), BF16)

        @pl.when(i == 0)
        def _():
            stats_ref[0] = lse_ref[...]

        for g in range(group):
            cols = slice(g * hdim, (g + 1) * hdim)
            product = d_ref[:, cols].astype(F32) * o_ref[:, cols].astype(F32)
            high = product.astype(BF16)
            low = (product - high.astype(F32)).astype(BF16)
            delta = dot_nt(ones, high) + dot_nt(ones, low)
            stats_ref[1, pl.ds(i * group + g, 1), :] = delta[:1]

    block = pl.BlockSpec((rows, group * hdim), lambda i: (0, i))
    size = rows * heads * hdim
    (stats,) = call(
        body,
        heads // group,
        (lse, output, d),
        [pl.BlockSpec((heads, rows), lambda i: (0, 0)), block, block],
        [jax.ShapeDtypeStruct((2, heads, rows), F32)],
        [pl.BlockSpec((2, heads, rows), lambda i: (0, 0, 0))],
        (2 * size, 4 * size, 0),
        after,
    )
    return stats


def second_pack(q, k, v, d, stats, first, heads, hdim):
    rows = q.shape[0]
    cols = heads * hdim
    count = stats.shape[1]
    half = count // 2
    split = cols - rows

    def body(ins, outs):
        q_ref, k_ref, v_ref, d_ref, stats_ref = ins
        fill(*sides()[:2], *outs, q_ref, k_ref, v_ref, d_ref)
        for n in range(2):
            high = stats_ref[n].astype(BF16)
            low = (stats_ref[n] - high.astype(F32)).astype(BF16)
            for ref in outs:
                ref[n, rows : rows + count, :rows] = high
                ref[n, rows : rows + count, rows:] = low[:, :split]
                ref[n, rows + count :, : rows - split] = low[:half, split:]
                ref[n, rows + count :, rows - split :] = low[half:, split:]

    block = pl.BlockSpec((rows, cols), lambda i: (0, first // heads))
    shape = jax.ShapeDtypeStruct((2, rows + count + half, cols), BF16)
    size = rows * cols
    return call(
        body,
        1,
        (q, k, v, d, stats),
        [block] * 4 + [pl.BlockSpec(stats.shape, lambda i: (0, 0, 0))],
        [shape] * 2,
        [pl.BlockSpec(shape.shape, lambda i: (0, 0, 0))] * 2,
        (0, 16 * size, 0),
    )


def read_stats(come_a, come_b, stats):
    _, count, rows = stats.shape
    cols = come_a.shape[2]
    half = count // 2
    split = cols - rows

    def body(ins, outs):
        for sent, out in zip(ins, outs):
            for n in range(2):
                top = sent[n, :count, :].astype(F32)
                below = sent[n, count:, :].astype(F32)
                rest = jnp.concatenate([below[:, : rows - split], below[:, rows - split :]], axis=0)
                low = jnp.concatenate([top[:, rows:], rest], axis=1)
                out[n] = top[:, :rows] + low

    block = pl.BlockSpec((2, count + half, cols), lambda i: (0, rows // (count + half), 0))
    return call(
        body,
        1,
        (come_a, come_b),
        [block] * 2,
        [jax.ShapeDtypeStruct(stats.shape, F32)] * 2,
        [pl.BlockSpec(stats.shape, lambda i: (0, 0, 0))] * 2,
        (0, 4 * count * rows, 0),
        vmem=4 << 20,
    )


def prob_terms(k, v, q, d, lse, delta, causal=False):
    scale = 1.0 / math.sqrt(q.shape[1])
    prob = jnp.exp2(dot_nt(k, q) * (scale * LOG2E) - lse * LOG2E)
    if causal:
        key_row = lax.broadcasted_iota(jnp.int32, prob.shape, 0)
        query_row = lax.broadcasted_iota(jnp.int32, prob.shape, 1)
        prob = jnp.where(key_row <= query_row, prob, 0.0)
    dscore = prob * (dot_nt(v, d) * scale - delta * scale)
    return prob.astype(BF16), dscore.astype(BF16)


def own_block(q, k, v, d, stats, first, heads, packed, after):
    rows = q.shape[0]
    hdim = q.shape[1] // stats.shape[1]
    group = math.gcd(first, heads, 4)
    cols = group * hdim

    def body(ins, outs):
        q_ref, k_ref, v_ref, d_ref, stats_ref = ins
        gq_ref, gk_ref, gv_ref, token_ref = outs[:4]
        token_ref[...] = jnp.zeros_like(token_ref)
        if packed:
            fill(*sides()[:2], *outs[4:], q_ref, k_ref, v_ref, d_ref)
        for g in range(group):
            at = slice(g * hdim, (g + 1) * hdim)
            h = first % ROWS + pl.program_id(0) * group + g
            qh, kh, vh, dh = q_ref[:, at], k_ref[:, at], v_ref[:, at], d_ref[:, at]
            lse = stats_ref[0, pl.ds(h, 1), :]
            delta = stats_ref[1, pl.ds(h, 1), :]
            prob, dscore = prob_terms(kh, vh, qh, dh, lse, delta, True)
            gq_ref[:, at] = dot_tn(dscore, kh)
            gk_ref[:, at] = dot_nn(dscore, qh)
            gv_ref[:, at] = dot_nn(prob, dh)

    block = pl.BlockSpec((rows, cols), lambda i: (0, first // group + i))
    out = pl.BlockSpec((rows, cols), lambda i: (0, i))
    sent = pl.BlockSpec((2, rows, cols), lambda i: (0, 0, i))
    shape = jax.ShapeDtypeStruct((rows, heads * hdim), F32)
    sent_shape = jax.ShapeDtypeStruct((2, rows, heads * hdim), BF16)
    size = rows * heads * hdim
    results = call(
        body,
        heads // group,
        (q, k, v, d, stats),
        [block] * 4 + [pl.BlockSpec((2, ROWS, rows), lambda i: (0, first // ROWS, 0))],
        [shape] * 3 + [TOKEN] + ([sent_shape] * 2 if packed else []),
        [out] * 3 + [TOKEN_SPEC] + ([sent] * 2 if packed else []),
        (10 * rows * size, 28 * size, heads * rows * rows),
        after,
        vmem=OWN_VMEM,
    )
    return results[:3], results[3:4], results[4:]


def chunk_grads(q, k, v, d, stats, come_a, come_b, astats, bstats, own, outs, first, heads, after):
    rows, width = q.shape
    hdim = width // stats.shape[1]
    group = math.gcd(first, heads, 4)
    cols = group * hdim

    def body(ins, results):
        q_ref, k_ref, v_ref, d_ref, stats_ref, a_ref, b_ref, astats_ref, bstats_ref = ins[:9]
        pq_ref, pk_ref, pv_ref = ins[9:12]
        gq_ref, gk_ref, gv_ref, token_ref = results
        token_ref[...] = jnp.zeros_like(token_ref)
        _, _, come_a, come_b = sides()

        def head(g):
            return slice(g * hdim, (g + 1) * hdim), first % ROWS + pl.program_id(0) * group + g

        def keys_side(g, sent_ref, sent_stats):
            at, h = head(g)
            qh, dh = sent_ref[0, :, at], sent_ref[1, :, at]
            lse = sent_stats[0, pl.ds(h, 1), :]
            delta = sent_stats[1, pl.ds(h, 1), :]
            prob, dscore = prob_terms(k_ref[:, at], v_ref[:, at], qh, dh, lse, delta)
            return dot_nn(dscore, qh), dot_nn(prob, dh)

        def queries_side(g, sent_ref):
            at, h = head(g)
            kh, vh = sent_ref[0, :, at], sent_ref[1, :, at]
            lse = stats_ref[0, pl.ds(h, 1), :]
            delta = stats_ref[1, pl.ds(h, 1), :]
            _, dscore = prob_terms(kh, vh, q_ref[:, at], d_ref[:, at], lse, delta)
            return dot_tn(dscore, kh)

        def joined(part, at):
            return jnp.concatenate([a_ref[part, :, at], b_ref[part, :, at]], axis=0)

        def keys_only():
            for g in range(group):
                at, h = head(g)
                qh, dh = joined(0, at), joined(1, at)
                lse, delta = (
                    jnp.concatenate(
                        [astats_ref[n, pl.ds(h, 1), :], bstats_ref[n, pl.ds(h, 1), :]], axis=1
                    )
                    for n in range(2)
                )
                prob, dscore = prob_terms(k_ref[:, at], v_ref[:, at], qh, dh, lse, delta)
                gq_ref[:, at] = pq_ref[:, at].astype(BF16)
                gk_ref[:, at] = (pk_ref[:, at] + dot_nn(dscore, qh)).astype(BF16)
                gv_ref[:, at] = (pv_ref[:, at] + dot_nn(prob, dh)).astype(BF16)

        def both(q_ref, q_stats, k_ref):
            for g in range(group):
                at, _ = head(g)
                one_k, one_v = keys_side(g, q_ref, q_stats)
                gq_ref[:, at] = (pq_ref[:, at] + queries_side(g, k_ref)).astype(BF16)
                gk_ref[:, at] = (pk_ref[:, at] + one_k).astype(BF16)
                gv_ref[:, at] = (pv_ref[:, at] + one_v).astype(BF16)

        def queries_only():
            for g in range(group):
                at, h = head(g)
                kh, vh = joined(0, at), joined(1, at)
                lse = stats_ref[0, pl.ds(h, 1), :]
                delta = stats_ref[1, pl.ds(h, 1), :]
                _, dscore = prob_terms(kh, vh, q_ref[:, at], d_ref[:, at], lse, delta)
                gq_ref[:, at] = (pq_ref[:, at] + dot_tn(dscore, kh)).astype(BF16)
                gk_ref[:, at] = pk_ref[:, at].astype(BF16)
                gv_ref[:, at] = pv_ref[:, at].astype(BF16)

        no_a, no_b = jnp.logical_not(come_a), jnp.logical_not(come_b)
        pl.when(come_a & come_b)(keys_only)
        pl.when(come_a & no_b)(lambda: both(a_ref, astats_ref, b_ref))
        pl.when(no_a & come_b)(lambda: both(b_ref, bstats_ref, a_ref))
        pl.when(no_a & no_b)(queries_only)

    block = pl.BlockSpec((rows, cols), lambda i: (0, first // group + i))
    part = pl.BlockSpec((rows, cols), lambda i: (0, i))
    whole = pl.BlockSpec((2, ROWS, rows), lambda i: (0, first // ROWS, 0))
    sent = pl.BlockSpec((2, rows, cols), lambda i: (0, 0, i))
    size = rows * heads * hdim
    ins = (q, k, v, d, stats, come_a, come_b, astats, bstats) + tuple(own)
    in_specs = [block] * 4 + [whole, sent, sent, whole, whole] + [part] * 3
    aliases = {}
    if outs is not None:
        aliases = {len(ins) + n: n for n in range(3)}
        ins += tuple(outs)
        in_specs += [KEPT] * 3
    results = call(
        body,
        heads // group,
        ins,
        in_specs,
        [jax.ShapeDtypeStruct((rows, width), BF16)] * 3 + [TOKEN],
        [block] * 3 + [TOKEN_SPEC],
        (16 * rows * size, 34 * size, 2 * heads * rows * rows),
        after,
        aliases,
        vmem=CHUNK_VMEM,
    )
    return results[:3], results[3:]


def per_device(query, key, value, output, grad_out, lse):
    heads = lse.shape[0]
    hdim = query.shape[1] // heads
    count = lax.axis_size("ctx")
    near = count // 4
    way_a = [(s, (s + (near if s % 2 == 0 else -near)) % count) for s in range(count)]
    way_b = [(s, (s + (-near if s % 2 == 0 else near)) % count) for s in range(count)]
    arrays = (query, key, value, grad_out)
    firsts = [sum(CHUNKS[:c]) for c in range(len(CHUNKS))]
    last = len(CHUNKS) - 1
    own, sent, come_a, come_b = {}, {}, {}, {}

    def prepare(c, packed, after):
        own[c], token, packs = own_block(*arrays, stats, firsts[c], CHUNKS[c], packed, after)
        if packed:
            sent[c] = packs
        return token

    def send(c, after):
        if c > last:
            return ()
        token = ()
        if after:
            sent[c], token = gate(sent[c], after)
        come_a[c] = lax.ppermute(sent[c][0], "ctx", way_a)
        come_b[c] = lax.ppermute(sent[c][1], "ctx", way_b)
        return token

    sent[0] = first_pack(*arrays, CHUNKS[0], hdim)
    send(0, ())
    stats = row_stats(lse, output, grad_out, sent[0][:1])
    second_sent = second_pack(*arrays, stats, firsts[1], CHUNKS[1], hdim)
    sent[1] = second_sent
    send(1, ())
    token = prepare(2, True, second_sent[:1])
    token = send(2, (come_a[0], come_b[0], *token))
    token = prepare(0, False, token)
    token = prepare(1, False, token)
    for c in range(3, last + 1):
        token = prepare(c, True, token)
    astats, bstats = read_stats(come_a[1], come_b[1], stats)
    token = send(3, (astats, *token))
    outs, done = None, ()
    for c in range(last + 1):
        if c > 1:
            token = send(c + 2, (come_a[c], come_b[c], *done))
        outs, done = chunk_grads(
            *arrays, stats, come_a[c], come_b[c], astats, bstats, own[c], outs, firsts[c],
            CHUNKS[c], token,
        )
        token = ()
    return tuple(outs)


def solution(mesh):
    in_specs = (
        P(("rep", "ctx"), None),
        P(("rep", "ctx"), None),
        P(("rep", "ctx"), None),
        P(("rep", "ctx"), None),
        P(("rep", "ctx"), None),
        P(None, ("rep", "ctx")),
    )
    out_specs = (P(("rep", "ctx"), None), P(("rep", "ctx"), None), P(("rep", "ctx"), None))
    return jax.shard_map(
        per_device, mesh=mesh, in_specs=in_specs, out_specs=out_specs, check_vma=False
    )
```
